128 devices in a mesh: space: 32 (over z, x, core), mode: 4 (over y).
Axes of the slice: x: 4, y: 4, z: 4, core: 2. Of those that a mesh axis runs over, the one named last changes fastest.
Arguments:
- probe: float32 [8, 2, 2048, 4096], P('mode', None, 'space'), may hold values from -6 to 6
- specimen: bfloat16 [2, 2, 2048, 4096], P(None, None, 'space', 'mode'), may hold values from -4 to 4
- kernels: float32 [2, 2, 24], replicated, may hold values from -0.9 to 0.9
Outputs:
- exit_wave: float32 [8, 2, 2048, 4096], P('mode', None, 'space')
The draws below stay inside these ranges and needn't reach their ends.
All inputs are finite; a program needn't handle non-finite values.
Results may differ from the reference program's by a relative error of at most 0.0003.
Values may be sent and summed in bfloat16 or wider, within the bound.
No kernel may reach another device: no remote copies, remote signals or barrier semaphores. Data moves between devices by JAX's collectives and lax.ppermute only.
A program may use at most 64 MiB of HBM per device.

```python
import jax
import jax.numpy as jnp
from jax import lax

N = 4096
MODES = 8
TAPS = 24
SLICES = 2
NROWS = 2048


def block_scale(own_key, shape, split, smallest, top_value):
    def one(axis_at, shards_of):
        draws = jax.random.uniform(jax.random.fold_in(jax.random.fold_in(own_key, 6), axis_at), (shards_of,), jnp.float32, smallest / len(split), top_value / len(split))
        return jnp.repeat(jnp.exp(draws), shape[axis_at] // shards_of).reshape((-1,) + (1,) * (len(shape) - axis_at - 1))

    level = one(*split[0])
    for cut in split[1:]:
        level = level * one(*cut)
    return level


def scatter_about(rng, shape, deviation, limit, pieces=(), held_as=jnp.bfloat16):
    array = deviation * jax.random.normal(rng, shape, jnp.float32)
    if pieces:
        array = array * block_scale(rng, shape, pieces, -0.22, 0.18)
    return jnp.clip(array, -limit, limit).astype(held_as)


def setup_inputs(seed: int = 0) -> dict:
    key_of = jax.random.split(jax.random.key(seed), 4)
    probe = scatter_about(key_of[0], (MODES, 2, NROWS, N), 1.0, 6.0, ((0, 4), (2, 32)), jnp.float32)
    specimen = scatter_about(key_of[1], (SLICES, 2, NROWS, N), 0.7, 4.0, ((2, 32), (3, 4)))
    kernels = scatter_about(key_of[2], (2, 2, TAPS), 0.144, 0.9, (), jnp.float32)
    return {"probe": probe, "specimen": specimen, "kernels": kernels}


def correlate(f_real, f_imag, k_real, k_imag, axis):
    length = f_real.shape[axis]
    half_taps = TAPS // 2
    widths = [(0, 0)] * f_real.ndim
    widths[axis] = (half_taps, TAPS - 1 - half_taps)
    pad_real = jnp.pad(f_real, widths)
    pad_imag = jnp.pad(f_imag, widths)
    out_real = jnp.zeros_like(f_real)
    out_imag = jnp.zeros_like(f_imag)
    for offset in range(TAPS):
        sl_real = lax.slice_in_dim(pad_real, offset, offset + length, axis=axis)
        sl_imag = lax.slice_in_dim(pad_imag, offset, offset + length, axis=axis)
        out_real = out_real + k_real[offset] * sl_real - k_imag[offset] * sl_imag
        out_imag = out_imag + k_real[offset] * sl_imag + k_imag[offset] * sl_real
    return out_real, out_imag


def reference(probe, specimen, kernels):
    def one_mode(field):
        w_real = field[0]
        w_imag = field[1]
        for layer in range(SLICES):
            t_real = specimen[layer, 0].astype(jnp.float32)
            t_imag = specimen[layer, 1].astype(jnp.float32)
            x_real = w_real * t_real - w_imag * t_imag
            x_imag = w_real * t_imag + w_imag * t_real
            x_real, x_imag = correlate(x_real, x_imag, kernels[0, 0], kernels[0, 1], 0)
            w_real, w_imag = correlate(x_real, x_imag, kernels[1, 0], kernels[1, 1], 1)
        return jnp.stack([w_real, w_imag])

    return lax.map(one_mode, probe)
```

```python
import functools

import jax
import jax.numpy as jnp
from jax import lax
from jax.experimental import pallas as pl
from jax.experimental.pallas import tpu as pltpu
from jax.sharding import PartitionSpec as P

TAPS = 24
HALF = TAPS // 2
LANES = 128
OUTER = 24
INNER = 16
PIECES = 4
MODE, ODD, UP, DOWN = range(4)
CHUNK = 512
GROUP = 4
f32 = jnp.float32
bf16 = jnp.bfloat16
VMEM = pl.BlockSpec(memory_space=pltpu.VMEM)
SMEM = pl.BlockSpec(memory_space=pltpu.SMEM)
HBM = pl.BlockSpec(memory_space=pltpu.HBM)


def in_hbm(x):
    return pltpu.with_memory_space_constraint(x, pltpu.HBM)


def in_vmem(x):
    return pltpu.with_memory_space_constraint(x, pltpu.VMEM)


def split(x):
    high = x.astype(bf16)
    return high, (x - high.astype(f32)).astype(bf16)


def look_up(tap, kernels, axis):
    real = jnp.zeros(tap.shape, f32)
    imag = jnp.zeros(tap.shape, f32)
    for t in range(TAPS):
        here = tap == t
        real = jnp.where(here, kernels[axis, 0, t], real)
        imag = jnp.where(here, kernels[axis, 1, t], imag)
    return real, imag


def position(index, own, edge):
    outer = index >= 2 * own
    line = jnp.where(outer, index - 2 * own, index)
    size = jnp.where(outer, 2 * edge, own)
    imag = line >= size
    line = jnp.where(imag, line - size, line)
    return jnp.where(outer, jnp.where(line < edge, line - edge, line - edge + own), line), imag


def row_band(kernels, own, out_edge, in_edge):
    shape = (2 * own + 4 * out_edge, 2 * own + 4 * in_edge)
    to, to_imag = position(lax.broadcasted_iota(jnp.int32, shape, 0), own, out_edge)
    at, at_imag = position(lax.broadcasted_iota(jnp.int32, shape, 1), own, in_edge)
    real, imag = look_up(at - to + HALF, kernels, 0)
    return split(jnp.where(to_imag == at_imag, real, jnp.where(to_imag, imag, -imag)))


def column_rows(source, is_imag, kernels):
    j = lax.broadcasted_iota(jnp.int32, source.shape, 1)
    real, imag = look_up(source - j + HALF, kernels, 1)
    left = jnp.where(is_imag, -imag, real)
    right = jnp.where(is_imag, real, imag)
    return split(left), split(right)


def tail_source(lane):
    is_imag = (lane >= 32) & (lane < 96)
    plain = jnp.where(is_imag, lane ^ 64, lane)
    source = jnp.where(plain < 64, plain + LANES, plain - LANES)
    inside = (plain < HALF) | (plain >= LANES - HALF)
    return jnp.where(inside, source, 1 << 20), is_imag


def edges_kernel(for_odd, place, probe, out, held, sems):
    odd = place[ODD]
    row = (odd if for_odd else 1 - odd) * (probe.shape[2] - OUTER)
    rows = pl.ds(pl.multiple_of(row, 8), OUTER)
    steps = [(m, p) for m in range(probe.shape[0]) for p in range(2)]
    takes = [pltpu.make_async_copy(probe.at[m, p, rows], held.at[m, p], sems.at[0, m, p]) for m, p in steps]
    gives = [pltpu.make_async_copy(held.at[m, p], out.at[m, p], sems.at[1, m, p]) for m, p in steps]
    for take in takes:
        take.start()
    for take, give in zip(takes, gives):
        take.wait()
        give.start()
    for give in gives:
        give.wait()


def edges(for_odd, place, probe):
    shape = (*probe.shape[:2], OUTER, probe.shape[3])
    return pl.pallas_call(
        functools.partial(edges_kernel, for_odd),
        out_shape=jax.ShapeDtypeStruct(shape, f32),
        in_specs=[SMEM, HBM],
        out_specs=HBM,
        scratch_shapes=[pltpu.VMEM(shape, f32), pltpu.SemaphoreType.DMA((2, shape[0], 2))],
        compiler_params=pltpu.CompilerParams(vmem_limit_bytes=4 * 1024 * 1024),
        name="edges_cross" if for_odd else "edges_inner",
    )(place, in_hbm(probe))


def prepare_kernel(kernels, row0h, row0l, row1h, row1l, col):
    own = row1h.shape[0] // 2
    row0h[...], row0l[...] = row_band(kernels, own, INNER, OUTER)
    row1h[...], row1l[...] = row_band(kernels, own, 0, INNER)
    lane = lax.broadcasted_iota(jnp.int32, (LANES, LANES), 0)
    for plane in range(2):
        left, right = column_rows(lane, jnp.full(lane.shape, plane == 1), kernels)
        for group, part in ((0, 0), (1, 0), (2, 1)):
            at = pl.ds((2 * group + plane) * LANES, LANES)
            col[at, :LANES] = left[part]
            col[at, LANES:] = right[part]
    source, is_imag = tail_source(lane)
    left, right = column_rows(source, is_imag, kernels)
    col[6 * LANES : 7 * LANES, :LANES] = left[0]
    col[6 * LANES : 7 * LANES, LANES:] = right[0]
    moved = (lane + LANES - 32) & (LANES - 1)
    source_moved, imag_moved = tail_source(moved)
    left_moved, right_moved = column_rows(source_moved, imag_moved, kernels)
    here = source < (1 << 19)
    col[7 * LANES :, :LANES] = jnp.where(here, left[0].astype(f32), left_moved[1].astype(f32)).astype(bf16)
    col[7 * LANES :, LANES:] = jnp.where(here, right[0].astype(f32), right_moved[1].astype(f32)).astype(bf16)


def prepare(kernels, own):
    mid = 2 * own + 4 * INNER
    shapes = [(mid, 2 * own + 4 * OUTER)] * 2 + [(2 * own, mid)] * 2 + [(8 * LANES, 2 * LANES)]
    return pl.pallas_call(
        prepare_kernel,
        out_shape=[pltpu.VMEM(s, bf16) for s in shapes],
        in_specs=[SMEM],
        out_specs=[VMEM] * 5,
        compiler_params=pltpu.CompilerParams(vmem_limit_bytes=8 * 1024 * 1024),
        name="prepare",
    )(kernels)


def dot(a, b):
    return jnp.dot(a, b, preferred_element_type=f32)


def row_stage(x_high, x_low, band_high, band_low):
    n = band_high.shape[0]
    both = dot(jnp.concatenate([band_high[...], band_low[...]], axis=0), x_high)
    return both[:n] + both[n:] + dot(band_high[...], x_low)


def product(f_real, f_imag, t_real, t_imag):
    return f_real * t_real - f_imag * t_imag, f_real * t_imag + f_imag * t_real


def lanes(block):
    return slice(block * LANES, (block + 1) * LANES)


def block_rows(j, rows, n=1):
    return slice(j * rows, (j + n) * rows)


def put(blocks, j, planes):
    rows, width = planes[0].shape
    for p, plane in enumerate(planes):
        high, low = split(plane)
        for b in range(width // LANES):
            at = block_rows(j + b, rows)
            blocks[at, lanes(p)] = high[:, lanes(b)]
            blocks[at, lanes(p + 2)] = low[:, lanes(b)]


def joined(place, piece):
    return jnp.where(lax.rem(place[MODE] + piece + PIECES - 1, PIECES) == PIECES - 1, 0.0, 1.0)


def column_stage(place, blocks, tails, col, js, rows, emit):
    total = blocks.shape[0] // rows
    per = total // PIECES
    lane = lax.broadcasted_iota(jnp.int16, (rows, LANES), 1)
    plain = lane & 63
    middle = (lane >= 32) & (lane < 96)
    used = (plain < HALF) | (plain >= 64 - HALF)

    def beside(j, step, k):
        x = blocks[block_rows((j + step) % total, rows), lanes(k)]
        if (j + (step > 0)) % per:
            return x
        keep = joined(place, (j // per - (step < 0)) % PIECES)
        return (x.astype(f32) * keep).astype(bf16)

    for n, j in enumerate(js):
        side = [jnp.where(lane < 64, beside(j, 1, k), beside(j, -1, k)) for k in range(4)]
        high = jnp.where(middle, pltpu.roll(side[1], 64, 1), side[0])
        low = jnp.where(middle, pltpu.roll(side[3], 64, 1), side[2])
        tails[block_rows(n, rows), lanes(0)] = high
        tails[block_rows(n, rows), lanes(1)] = jnp.where(used, low, pltpu.roll(high, 32, 1))
    two = 2 * LANES
    done = 0
    while done < len(js):
        first = js[done] % total
        n = min(len(js) - done, total - first, GROUP)
        at = block_rows(first, rows, n)
        main = blocks[at, :two]
        result = dot(main, col[:two, :]) + dot(blocks[at, two:], col[two : 2 * two, :])
        result = result + dot(main, col[2 * two : 3 * two, :]) + dot(tails[block_rows(done, rows, n), :], col[3 * two :, :])
        for b in range(n):
            part = result[block_rows(b, rows)]
            emit(first + b, part[:, :LANES], part[:, LANES:])
        done += n


def chunks(width):
    return [slice(c, c + CHUNK) for c in range(0, width, CHUNK)]


def keep_columns(lines, rows):
    def emit(j, real, imag):
        for p, plane in enumerate((real, imag)):
            for k, part in enumerate(split(plane)):
                lines[k, p * rows : (p + 1) * rows, lanes(j)] = part

    return emit


def piece_columns(place, q, piece):
    return pl.ds(pl.multiple_of(lax.rem(place[MODE] + q + PIECES - 1, PIECES) * piece, piece), piece)


def own_product(fields, spec, blocks, q, at, piece):
    cells = slice(q * piece + at.start, q * piece + at.stop)
    planes = product(fields[0, :, at], fields[1, :, at], *(x[:, at].astype(f32) for x in spec))
    put(blocks, cells.start // LANES, planes)


def near_kernel(place, probe, left, own_spec, right, col, blocks, lines, fields, tails, sems):
    specs = (left, own_spec, right)
    modes, _, rows, width = probe.shape
    piece = width // PIECES
    per = piece // LANES

    def fetch(m, q):
        return pltpu.make_async_copy(probe.at[m, :, :, piece_columns(place, q, piece)], fields.at[m, q], sems.at[m, q])

    order = [(m, q) for m in range(modes) for q in range(len(specs))]
    for m, q in order:
        fetch(m, q).start()
    for m in range(modes):
        for q, spec in enumerate(specs):
            fetch(m, q).wait()
            for at in chunks(piece):
                own_product(fields.at[m, q], [spec.at[0, p] for p in range(2)], blocks.at[m], q, at, piece)
        js = list(range(1, len(specs) * per - 1))
        column_stage(place, blocks.at[m], tails.at[m], col, js, rows, keep_columns(lines.at[m], rows))


def near(place, probe, specs, col):
    modes, _, own, width = probe.shape
    args = [in_hbm(probe)] + [in_vmem(x) for x in (*specs, col)]
    piece = width // PIECES
    return pl.pallas_call(
        near_kernel,
        out_shape=[
            pltpu.VMEM((modes, width // LANES * own, 4 * LANES), bf16),
            pltpu.VMEM((modes, 2, 2 * own, width), bf16),
        ],
        in_specs=[SMEM, HBM] + [VMEM] * (len(args) - 1),
        out_specs=[VMEM] * 2,
        scratch_shapes=[
            pltpu.VMEM((modes, len(specs), 2, own, piece), f32),
            pltpu.VMEM((modes, len(specs) * piece // LANES * own, 2 * LANES), bf16),
            pltpu.SemaphoreType.DMA((modes, len(specs))),
        ],
        compiler_params=pltpu.CompilerParams(vmem_limit_bytes=20 * 1024 * 1024),
        cost_estimate=pl.CostEstimate(flops=6 * 10**9, bytes_accessed=10**7, transcendentals=0),
        name="near",
    )(place, *args)


def first_kernel(place, probe, cross, inner, near_cross, near_inner, far_cross, far_inner, far_spec, high, low, col, _b, _l, *refs):
    wave, blocks, lines, strips, fields, edge_rows, outer, outer_lines, tails, outer_tails, sems, strip_sems = refs
    modes, _, rows, width = probe.shape
    piece = width // PIECES
    per = piece // LANES
    far = PIECES - 1
    edge = 2 * OUTER
    odd = place[ODD]
    keep = [place[UP].astype(f32), place[DOWN].astype(f32)]

    def fetch(m, q):
        at = piece_columns(place, q, piece)
        copies = [
            pltpu.make_async_copy(source.at[m, :, :, at], edge_rows.at[to, m, q], sems.at[k, m, q])
            for k, (source, to) in enumerate(((cross, odd), (inner, 1 - odd)))
        ]
        if q == far:
            copies.append(pltpu.make_async_copy(probe.at[m, :, :, at], fields.at[m], sems.at[2, m, 0]))
        return copies

    strip_copies = []
    for k, (source, to, q) in enumerate(((near_cross, odd, 0), (near_inner, 1 - odd, 0), (far_cross, odd, far), (far_inner, 1 - odd, far))):
        strip_copies.append(pltpu.make_async_copy(source, strips.at[to, q : q + source.shape[0]], strip_sems.at[k]))
    order = [far] + list(range(far))
    for copy in strip_copies:
        copy.start()
    for m in range(modes):
        for q in order:
            for copy in fetch(m, q):
                copy.start()
    for copy in strip_copies:
        copy.wait()
    for m in range(modes):
        for q in order:
            for copy in fetch(m, q):
                copy.wait()
            for at in chunks(piece):
                if q == far:
                    own_product(fields.at[m], (far_spec.at[0], far_spec.at[1]), blocks.at[m], q, at, piece)
                planes = [
                    product(*(edge_rows[e, m, q, p, :, at] for p in range(2)), *(strips[e, q, p, INNER:, at].astype(f32) * keep[e] for p in range(2)))
                    for e in range(2)
                ]
                put(outer.at[m], (q * piece + at.start) // LANES, [jnp.concatenate([planes[0][p], planes[1][p]], axis=0) for p in range(2)])
        js = list(range(far * per - 1, PIECES * per + 1))
        column_stage(place, blocks.at[m], tails.at[m], col, js, rows, keep_columns(lines.at[m], rows))
        column_stage(place, outer.at[m], outer_tails.at[m], col, list(range(PIECES * per)), edge, keep_columns(outer_lines.at[m], edge))
        for at in chunks(width):
            x = [jnp.concatenate([lines[m, k, :, at], outer_lines[m, k, :, at]], axis=0) for k in range(2)]
            wave[m, :, at] = row_stage(*x, high, low)


def first_slice(place, probe, halos, strips, far, bands, blocks, lines):
    modes, _, own, width = probe.shape
    piece = width // PIECES
    anywhere = [*halos, *strips]
    args = [in_hbm(probe), *anywhere] + [in_vmem(x) for x in (far, *bands, blocks, lines)]
    edge = 2 * OUTER
    total = width // LANES
    return pl.pallas_call(
        first_kernel,
        out_shape=[
            pltpu.VMEM((modes, 2 * own + 4 * INNER, width), f32),
            pltpu.VMEM(blocks.shape, bf16),
            pltpu.VMEM(lines.shape, bf16),
            pltpu.VMEM((2, PIECES, *strips[0].shape[1:]), bf16),
        ],
        in_specs=[SMEM, HBM] + [pl.BlockSpec(memory_space=pl.ANY)] * len(anywhere) + [VMEM] * (len(args) - 1 - len(anywhere)),
        out_specs=[VMEM] * 4,
        input_output_aliases={len(args) - 1: 1, len(args): 2},
        scratch_shapes=[
            pltpu.VMEM((modes, 2, own, piece), f32),
            pltpu.VMEM((2, modes, PIECES, 2, OUTER, piece), f32),
            pltpu.VMEM((modes, total * edge, 4 * LANES), bf16),
            pltpu.VMEM((modes, 2, 2 * edge, width), bf16),
            pltpu.VMEM((modes, (total // PIECES + 2) * own, 2 * LANES), bf16),
            pltpu.VMEM((modes, total * edge, 2 * LANES), bf16),
            pltpu.SemaphoreType.DMA((3, modes, PIECES)),
            pltpu.SemaphoreType.DMA((4,)),
        ],
        compiler_params=pltpu.CompilerParams(vmem_limit_bytes=28 * 1024 * 1024),
        name="first_slice",
    )(place, *args)


def second_kernel(place, wave, left, own_spec, right, far_spec, strips, high, low, col, out, blocks, tails, stage, sems):
    modes, _, rows, width = out.shape
    piece = width // PIECES
    per = piece // LANES
    keep = [place[UP].astype(f32), place[DOWN].astype(f32)]
    specs = [[x.at[1, p] for p in range(2)] for x in (left, own_spec, right)] + [[far_spec.at[0], far_spec.at[1]]]

    def leave(m, q):
        at = slice(q * piece, (q + 1) * piece)
        return pltpu.make_async_copy(stage.at[m, :, :, at], out.at[m, :, :, piece_columns(place, q, piece)], sems.at[m, q])

    for m in range(modes):
        for q in range(PIECES):
            for at in chunks(piece):
                cells = slice(q * piece + at.start, q * piece + at.stop)
                inside = product(wave[m, :rows, cells], wave[m, rows : 2 * rows, cells], *(x[:, at].astype(f32) for x in specs[q]))
                edge = [jnp.concatenate([strips[e, q, p, :INNER, at].astype(f32) * keep[e] for e in range(2)], axis=0) for p in range(2)]
                first = 2 * rows
                outside = product(wave[m, first : first + 2 * INNER, cells], wave[m, first + 2 * INNER :, cells], *edge)
                result = row_stage(*split(jnp.concatenate([*inside, *outside], axis=0)), high, low)
                put(blocks.at[m], cells.start // LANES, (result[:rows], result[rows:]))

        def emit(j, real, imag, m=m):
            stage[m, 0, :, lanes(j)] = real
            stage[m, 1, :, lanes(j)] = imag
            if j % per == per - 1:
                leave(m, j // per).start()

        column_stage(place, blocks.at[m], tails.at[m], col, list(range(PIECES * per)), rows, emit)
    for m in range(modes):
        for q in range(PIECES):
            leave(m, q).wait()


def second_slice(place, wave, specs, strips, bands, own):
    modes, _, width = wave.shape
    args = [in_vmem(x) for x in (wave, *specs, strips, *bands)]
    shape = (modes, 2, own, width)
    total = width // LANES
    return pl.pallas_call(
        second_kernel,
        out_shape=jax.ShapeDtypeStruct(shape, f32),
        in_specs=[SMEM] + [VMEM] * len(args),
        out_specs=HBM,
        scratch_shapes=[
            pltpu.VMEM((modes, total * own, 4 * LANES), bf16),
            pltpu.VMEM((modes, total * own, 2 * LANES), bf16),
            pltpu.VMEM(shape, f32),
            pltpu.SemaphoreType.DMA((modes, PIECES)),
        ],
        compiler_params=pltpu.CompilerParams(vmem_limit_bytes=28 * 1024 * 1024),
        name="second_slice",
    )(place, *args)


def turn(x, axis, by):
    n = lax.axis_size(axis)
    return lax.ppermute(x, axis, [(i, (i + by) % n) for i in range(n)])


def swap(x, first):
    n = lax.axis_size("space")
    pairs = [(i, i + 1) for i in range(first, n - 1, 2)]
    return lax.ppermute(x, "space", pairs + [(j, i) for i, j in pairs])


def on_device(probe, specimen, kernels):
    own = probe.shape[2]
    space, mode = lax.axis_index("space"), lax.axis_index("mode")
    odd = space % 2
    place = jnp.stack([mode, odd, (space > 0).astype(jnp.int32), (space < lax.axis_size("space") - 1).astype(jnp.int32)])
    left, right = turn(specimen, "mode", 1), turn(specimen, "mode", -1)
    cross = swap(edges(True, place, probe), 1)
    inner = swap(edges(False, place, probe), 0)
    *bands0, band1h, band1l, col = prepare(kernels, own)
    left, right, col = lax.optimization_barrier((left, right, col))
    far0, far1 = turn(left[0], "mode", 1), turn(right[1], "mode", -1)

    def strips(specs):
        last = jnp.stack([jnp.concatenate([x[1][:, own - INNER :], x[0][:, own - OUTER :]], axis=1) for x in specs])
        first = jnp.stack([jnp.concatenate([x[1][:, :INNER], x[0][:, :OUTER]], axis=1) for x in specs])
        return swap(jnp.where(odd == 1, last, first), 1), swap(jnp.where(odd == 1, first, last), 0)

    left_here, right_here, inner = lax.optimization_barrier((left, right, inner))
    near_cross, near_inner = strips([left_here, specimen, right_here])
    blocks, lines = near(place, probe, [left, specimen, right], col)
    far0, far1, blocks, lines, near_inner = lax.optimization_barrier((far0, far1, blocks, lines, near_inner))
    far_cross, far_inner = strips([(far0, far1)])
    all_strips = (near_cross, near_inner, far_cross, far_inner)
    wave, _, _, edge_strips = first_slice(place, probe, (cross, inner), all_strips, far0, (*bands0, col), blocks, lines)
    specs = (left, specimen, right, far1)
    return second_slice(place, wave, specs, edge_strips, (band1h, band1l, col), own)


def solution(mesh):
    return jax.shard_map(
        on_device,
        mesh=mesh,
        in_specs=(P("mode", None, "space", None), P(None, None, "space", "mode"), P()),
        out_specs=P("mode", None, "space", None),
        check_vma=False,
    )
```

```python
import functools

import jax
import jax.numpy as jnp
from jax import lax
from jax.experimental import pallas as pl
from jax.experimental.pallas import tpu as pltpu
from jax.sharding import PartitionSpec as P

TAPS = 24
HALF = TAPS // 2
LANES = 128
OUTER = 24
INNER = 16
PIECES = 4
MODE, ODD, UP, DOWN = range(4)
CHUNK = 512
GROUP = 4
f32 = jnp.float32
bf16 = jnp.bfloat16
VMEM = pl.BlockSpec(memory_space=pltpu.VMEM)
SMEM = pl.BlockSpec(memory_space=pltpu.SMEM)
HBM = pl.BlockSpec(memory_space=pltpu.HBM)


def in_hbm(x):
    return pltpu.with_memory_space_constraint(x, pltpu.HBM)


def in_vmem(x):
    return pltpu.with_memory_space_constraint(x, pltpu.VMEM)


def split(x):
    high = x.astype(bf16)
    return high, (x - high.astype(f32)).astype(bf16)


def look_up(tap, kernels, axis):
    real = jnp.zeros(tap.shape, f32)
    imag = jnp.zeros(tap.shape, f32)
    for t in range(TAPS):
        here = tap == t
        real = jnp.where(here, kernels[axis, 0, t], real)
        imag = jnp.where(here, kernels[axis, 1, t], imag)
    return real, imag


def position(index, own, edge):
    outer = index >= 2 * own
    line = jnp.where(outer, index - 2 * own, index)
    size = jnp.where(outer, 2 * edge, own)
    imag = line >= size
    line = jnp.where(imag, line - size, line)
    return jnp.where(outer, jnp.where(line < edge, line - edge, line - edge + own), line), imag


def row_band(kernels, own, out_edge, in_edge):
    shape = (2 * own + 4 * out_edge, 2 * own + 4 * in_edge)
    to, to_imag = position(lax.broadcasted_iota(jnp.int32, shape, 0), own, out_edge)
    at, at_imag = position(lax.broadcasted_iota(jnp.int32, shape, 1), own, in_edge)
    real, imag = look_up(at - to + HALF, kernels, 0)
    return split(jnp.where(to_imag == at_imag, real, jnp.where(to_imag, imag, -imag)))


def column_rows(source, is_imag, kernels):
    j = lax.broadcasted_iota(jnp.int32, source.shape, 1)
    real, imag = look_up(source - j + HALF, kernels, 1)
    left = jnp.where(is_imag, -imag, real)
    right = jnp.where(is_imag, real, imag)
    return split(left), split(right)


def tail_source(lane):
    is_imag = (lane >= 32) & (lane < 96)
    plain = jnp.where(is_imag, lane ^ 64, lane)
    source = jnp.where(plain < 64, plain + LANES, plain - LANES)
    inside = (plain < HALF) | (plain >= LANES - HALF)
    return jnp.where(inside, source, 1 << 20), is_imag


def edges_kernel(for_odd, place, probe, out, held, sems):
    odd = place[ODD]
    row = (odd if for_odd else 1 - odd) * (probe.shape[2] - OUTER)
    rows = pl.ds(pl.multiple_of(row, 8), OUTER)
    steps = [(m, p) for m in range(probe.shape[0]) for p in range(2)]
    takes = [pltpu.make_async_copy(probe.at[m, p, rows], held.at[m, p], sems.at[0, m, p]) for m, p in steps]
    gives = [pltpu.make_async_copy(held.at[m, p], out.at[m, p], sems.at[1, m, p]) for m, p in steps]
    for take in takes:
        take.start()
    for take, give in zip(takes, gives):
        take.wait()
        give.start()
    for give in gives:
        give.wait()


def edges(for_odd, place, probe):
    shape = (*probe.shape[:2], OUTER, probe.shape[3])
    return pl.pallas_call(
        functools.partial(edges_kernel, for_odd),
        out_shape=jax.ShapeDtypeStruct(shape, f32),
        in_specs=[SMEM, HBM],
        out_specs=HBM,
        scratch_shapes=[pltpu.VMEM(shape, f32), pltpu.SemaphoreType.DMA((2, shape[0], 2))],
        compiler_params=pltpu.CompilerParams(vmem_limit_bytes=4 * 1024 * 1024),
        name="edges_cross" if for_odd else "edges_inner",
    )(place, in_hbm(probe))


def prepare_kernel(kernels, row0h, row0l, row1h, row1l, col):
    own = row1h.shape[0] // 2
    row0h[...], row0l[...] = row_band(kernels, own, INNER, OUTER)
    row1h[...], row1l[...] = row_band(kernels, own, 0, INNER)
    lane = lax.broadcasted_iota(jnp.int32, (LANES, LANES), 0)
    for plane in range(2):
        left, right = column_rows(lane, jnp.full(lane.shape, plane == 1), kernels)
        for group, part in ((0, 0), (1, 0), (2, 1)):
            at = pl.ds((2 * group + plane) * LANES, LANES)
            col[at, :LANES] = left[part]
            col[at, LANES:] = right[part]
    source, is_imag = tail_source(lane)
    left, right = column_rows(source, is_imag, kernels)
    col[6 * LANES : 7 * LANES, :LANES] = left[0]
    col[6 * LANES : 7 * LANES, LANES:] = right[0]
    moved = (lane + LANES - 32) & (LANES - 1)
    source_moved, imag_moved = tail_source(moved)
    left_moved, right_moved = column_rows(source_moved, imag_moved, kernels)
    here = source < (1 << 19)
    col[7 * LANES :, :LANES] = jnp.where(here, left[0].astype(f32), left_moved[1].astype(f32)).astype(bf16)
    col[7 * LANES :, LANES:] = jnp.where(here, right[0].astype(f32), right_moved[1].astype(f32)).astype(bf16)


def prepare(kernels, own):
    mid = 2 * own + 4 * INNER
    shapes = [(mid, 2 * own + 4 * OUTER)] * 2 + [(2 * own, mid)] * 2 + [(8 * LANES, 2 * LANES)]
    return pl.pallas_call(
        prepare_kernel,
        out_shape=[pltpu.VMEM(s, bf16) for s in shapes],
        in_specs=[SMEM],
        out_specs=[VMEM] * 5,
        compiler_params=pltpu.CompilerParams(vmem_limit_bytes=8 * 1024 * 1024),
        name="prepare",
    )(kernels)


def dot(a, b):
    return jnp.dot(a, b, preferred_element_type=f32)


def row_stage(x_high, x_low, band_high, band_low):
    n = band_high.shape[0]
    both = dot(jnp.concatenate([band_high[...], band_low[...]], axis=0), x_high)
    return both[:n] + both[n:] + dot(band_high[...], x_low)


def product(f_real, f_imag, t_real, t_imag):
    return f_real * t_real - f_imag * t_imag, f_real * t_imag + f_imag * t_real


def lanes(block):
    return slice(block * LANES, (block + 1) * LANES)


def block_rows(j, rows, n=1):
    return slice(j * rows, (j + n) * rows)


def put(blocks, j, planes):
    rows, width = planes[0].shape
    for p, plane in enumerate(planes):
        high, low = split(plane)
        for b in range(width // LANES):
            at = block_rows(j + b, rows)
            blocks[at, lanes(p)] = high[:, lanes(b)]
            blocks[at, lanes(p + 2)] = low[:, lanes(b)]


def joined(place, piece):
    return jnp.where(lax.rem(place[MODE] + piece + PIECES - 1, PIECES) == PIECES - 1, 0.0, 1.0)


def column_stage(place, blocks, tails, col, js, rows, emit):
    total = blocks.shape[0] // rows
    per = total // PIECES
    lane = lax.broadcasted_iota(jnp.int16, (rows, LANES), 1)
    plain = lane & 63
    middle = (lane >= 32) & (lane < 96)
    used = (plain < HALF) | (plain >= 64 - HALF)

    def beside(j, step, k):
        x = blocks[block_rows((j + step) % total, rows), lanes(k)]
        if (j + (step > 0)) % per:
            return x
        keep = joined(place, (j // per - (step < 0)) % PIECES)
        return (x.astype(f32) * keep).astype(bf16)

    for n, j in enumerate(js):
        side = [jnp.where(lane < 64, beside(j, 1, k), beside(j, -1, k)) for k in range(4)]
        high = jnp.where(middle, pltpu.roll(side[1], 64, 1), side[0])
        low = jnp.where(middle, pltpu.roll(side[3], 64, 1), side[2])
        tails[block_rows(n, rows), lanes(0)] = high
        tails[block_rows(n, rows), lanes(1)] = jnp.where(used, low, pltpu.roll(high, 32, 1))
    two = 2 * LANES
    done = 0
    while done < len(js):
        first = js[done] % total
        n = min(len(js) - done, total - first, GROUP)
        at = block_rows(first, rows, n)
        main = blocks[at, :two]
        result = dot(main, col[:two, :]) + dot(blocks[at, two:], col[two : 2 * two, :])
        result = result + dot(main, col[2 * two : 3 * two, :]) + dot(tails[block_rows(done, rows, n), :], col[3 * two :, :])
        for b in range(n):
            part = result[block_rows(b, rows)]
            emit(first + b, part[:, :LANES], part[:, LANES:])
        done += n


def chunks(width):
    return [slice(c, c + CHUNK) for c in range(0, width, CHUNK)]


def keep_columns(lines, rows):
    def emit(j, real, imag):
        for p, plane in enumerate((real, imag)):
            for k, part in enumerate(split(plane)):
                lines[k, p * rows : (p + 1) * rows, lanes(j)] = part

    return emit


def piece_columns(place, q, piece):
    return pl.ds(pl.multiple_of(lax.rem(place[MODE] + q + PIECES - 1, PIECES) * piece, piece), piece)


def own_product(fields, spec, blocks, q, at, piece):
    cells = slice(q * piece + at.start, q * piece + at.stop)
    planes = product(fields[0, :, at], fields[1, :, at], *(x[:, at].astype(f32) for x in spec))
    put(blocks, cells.start // LANES, planes)


def own_kernel(tasks, edges_too, place, probe, *refs):
    n = 1 + max(q for _, pieces, _ in tasks for q in pieces)
    specs, col = refs[:n], refs[n]
    if edges_too:
        cross, inner = refs[n + 1 : n + 3]
        blocks, lines, edge_rows, fields, tails, sems, edge_sems = refs[n + 5 :]
    else:
        blocks, lines, fields, tails, sems = refs[n + 1 :]
    modes, _, rows, width = probe.shape
    piece = width // PIECES
    odd = place[ODD]

    def fetch(k, m, q):
        return pltpu.make_async_copy(probe.at[m, :, :, piece_columns(place, q, piece)], fields.at[k], sems.at[k])

    order = [(m, q) for m, pieces, _ in tasks for q in pieces]
    for k, (m, q) in enumerate(order):
        fetch(k, m, q).start()
    copies = []
    if edges_too:
        for m in range(modes):
            for q in range(PIECES):
                at = piece_columns(place, q, piece)
                for e, (source, to) in enumerate(((cross, odd), (inner, 1 - odd))):
                    copies.append(pltpu.make_async_copy(source.at[m, :, :, at], edge_rows.at[to, m, q], edge_sems.at[e, m, q]))
    for copy in copies:
        copy.start()
    k = 0
    for t, (m, pieces, js) in enumerate(tasks):
        for q in pieces:
            fetch(k, m, q).wait()
            spec = [specs[q].at[0, p] if q < PIECES - 1 else specs[q].at[p] for p in range(2)]
            for at in chunks(piece):
                own_product(fields.at[k], spec, blocks.at[m], q, at, piece)
            k += 1
        column_stage(place, blocks.at[m], tails.at[t], col, js, rows, keep_columns(lines.at[m], rows))
    for copy in copies:
        copy.wait()


def own_rows(tasks, place, probe, specs, col, halos=(), made=()):
    modes, _, own, width = probe.shape
    args = [in_hbm(probe)] + [in_vmem(x) for x in (*specs, col)] + [*halos] + [in_vmem(x) for x in made]
    piece = width // PIECES
    fetches = sum(len(pieces) for _, pieces, _ in tasks)
    longest = max(len(js) for _, _, js in tasks)
    out = [
        pltpu.VMEM((modes, width // LANES * own, 4 * LANES), bf16),
        pltpu.VMEM((modes, 2, 2 * own, width), bf16),
    ]
    scratch = [
        pltpu.VMEM((fetches, 2, own, piece), f32),
        pltpu.VMEM((len(tasks), longest * own, 2 * LANES), bf16),
        pltpu.SemaphoreType.DMA((fetches,)),
    ]
    if halos:
        out.append(pltpu.VMEM((2, modes, PIECES, 2, OUTER, piece), f32))
        scratch.append(pltpu.SemaphoreType.DMA((2, modes, PIECES)))
    first = 1 + len(args) - len(made)
    return pl.pallas_call(
        functools.partial(own_kernel, tasks, bool(halos)),
        out_shape=out,
        in_specs=[SMEM, HBM] + [VMEM] * (1 + len(specs)) + [pl.BlockSpec(memory_space=pl.ANY)] * len(halos) + [VMEM] * len(made),
        out_specs=[VMEM] * len(out),
        input_output_aliases={first + k: k for k in range(len(made))},
        scratch_shapes=scratch,
        compiler_params=pltpu.CompilerParams(vmem_limit_bytes=20 * 1024 * 1024),
        cost_estimate=pl.CostEstimate(flops=4 * 10**9, bytes_accessed=10**7, transcendentals=0),
        name="own_rest" if halos else "own_near",
    )(place, *args)


def first_kernel(place, edge_rows, strips_cross, strips_inner, high, low, col, lines, wave, strips, outer, outer_lines, outer_tails, strip_sems):
    _, modes, _, _, _, piece = edge_rows.shape
    width = PIECES * piece
    edge = 2 * OUTER
    odd = place[ODD]
    keep = [place[UP].astype(f32), place[DOWN].astype(f32)]
    strip_copies = [
        pltpu.make_async_copy(source, strips.at[to], strip_sems.at[to])
        for source, to in ((strips_cross, odd), (strips_inner, 1 - odd))
    ]
    for copy in strip_copies:
        copy.start()
    for copy in strip_copies:
        copy.wait()
    for m in range(modes):
        for q in range(PIECES):
            for at in chunks(piece):
                planes = [
                    product(*(edge_rows[e, m, q, p, :, at] for p in range(2)), *(strips[e, q, p, :, at].astype(f32) * keep[e] for p in range(2)))
                    for e in range(2)
                ]
                put(outer.at[m], (q * piece + at.start) // LANES, [jnp.concatenate([planes[0][p], planes[1][p]], axis=0) for p in range(2)])
        column_stage(place, outer.at[m], outer_tails.at[m], col, list(range(width // LANES)), edge, keep_columns(outer_lines.at[m], edge))
        for at in chunks(width):
            x = [jnp.concatenate([lines[m, k, :, at], outer_lines[m, k, :, at]], axis=0) for k in range(2)]
            wave[m, :, at] = row_stage(*x, high, low)


def first_slice(place, edge_rows, strips, bands, lines):
    modes = lines.shape[0]
    width = lines.shape[3]
    args = [in_vmem(edge_rows), *strips] + [in_vmem(x) for x in (*bands, lines)]
    edge = 2 * OUTER
    total = width // LANES
    return pl.pallas_call(
        first_kernel,
        out_shape=pltpu.VMEM((modes, bands[0].shape[0], width), f32),
        in_specs=[SMEM, VMEM] + [pl.BlockSpec(memory_space=pl.ANY)] * 2 + [VMEM] * (1 + len(bands)),
        out_specs=VMEM,
        scratch_shapes=[
            pltpu.VMEM((2, *strips[0].shape), bf16),
            pltpu.VMEM((modes, total * edge, 4 * LANES), bf16),
            pltpu.VMEM((modes, 2, 2 * edge, width), bf16),
            pltpu.VMEM((modes, total * edge, 2 * LANES), bf16),
            pltpu.SemaphoreType.DMA((2,)),
        ],
        compiler_params=pltpu.CompilerParams(vmem_limit_bytes=24 * 1024 * 1024),
        name="first_slice",
    )(place, *args)


def second_kernel(place, wave, left, own_spec, right, far_spec, strips_cross, strips_inner, high, low, col, out, blocks, tails, stage, strips, sems, strip_sems):
    modes, _, rows, width = out.shape
    piece = width // PIECES
    per = piece // LANES
    keep = [place[UP].astype(f32), place[DOWN].astype(f32)]
    specs = [[x.at[1, p] for p in range(2)] for x in (left, own_spec, right)] + [[far_spec.at[0], far_spec.at[1]]]
    odd = place[ODD]
    strip_copies = [
        pltpu.make_async_copy(source, strips.at[to], strip_sems.at[to])
        for source, to in ((strips_cross, odd), (strips_inner, 1 - odd))
    ]
    for copy in strip_copies:
        copy.start()
    for copy in strip_copies:
        copy.wait()

    def leave(m, q):
        at = slice(q * piece, (q + 1) * piece)
        return pltpu.make_async_copy(stage.at[m, :, :, at], out.at[m, :, :, piece_columns(place, q, piece)], sems.at[m, q])

    for m in range(modes):
        for q in range(PIECES):
            for at in chunks(piece):
                cells = slice(q * piece + at.start, q * piece + at.stop)
                inside = product(wave[m, :rows, cells], wave[m, rows : 2 * rows, cells], *(x[:, at].astype(f32) for x in specs[q]))
                edge = [jnp.concatenate([strips[e, q, p, :, at].astype(f32) * keep[e] for e in range(2)], axis=0) for p in range(2)]
                first = 2 * rows
                outside = product(wave[m, first : first + 2 * INNER, cells], wave[m, first + 2 * INNER :, cells], *edge)
                result = row_stage(*split(jnp.concatenate([*inside, *outside], axis=0)), high, low)
                put(blocks.at[m], cells.start // LANES, (result[:rows], result[rows:]))

        def emit(j, real, imag, m=m):
            stage[m, 0, :, lanes(j)] = real
            stage[m, 1, :, lanes(j)] = imag
            if j % per == per - 1:
                leave(m, j // per).start()

        column_stage(place, blocks.at[m], tails.at[m], col, list(range(PIECES * per)), rows, emit)
    for m in range(modes):
        for q in range(PIECES):
            leave(m, q).wait()


def second_slice(place, wave, specs, strips, bands, own):
    modes, _, width = wave.shape
    args = [*(in_vmem(x) for x in (wave, *specs)), *strips, *(in_vmem(x) for x in bands)]
    shape = (modes, 2, own, width)
    total = width // LANES
    return pl.pallas_call(
        second_kernel,
        out_shape=jax.ShapeDtypeStruct(shape, f32),
        in_specs=[SMEM] + [VMEM] * (1 + len(specs)) + [pl.BlockSpec(memory_space=pl.ANY)] * 2 + [VMEM] * len(bands),
        out_specs=HBM,
        scratch_shapes=[
            pltpu.VMEM((modes, total * own, 4 * LANES), bf16),
            pltpu.VMEM((modes, total * own, 2 * LANES), bf16),
            pltpu.VMEM(shape, f32),
            pltpu.VMEM((2, *strips[0].shape), bf16),
            pltpu.SemaphoreType.DMA((modes, PIECES)),
            pltpu.SemaphoreType.DMA((2,)),
        ],
        compiler_params=pltpu.CompilerParams(vmem_limit_bytes=28 * 1024 * 1024),
        name="second_slice",
    )(place, *args)


def turn(x, axis, by):
    n = lax.axis_size(axis)
    return lax.ppermute(x, axis, [(i, (i + by) % n) for i in range(n)])


def swap(x, first):
    n = lax.axis_size("space")
    pairs = [(i, i + 1) for i in range(first, n - 1, 2)]
    return lax.ppermute(x, "space", pairs + [(j, i) for i, j in pairs])


def on_device(probe, specimen, kernels):
    own = probe.shape[2]
    space, mode = lax.axis_index("space"), lax.axis_index("mode")
    odd = space % 2
    place = jnp.stack([mode, odd, (space > 0).astype(jnp.int32), (space < lax.axis_size("space") - 1).astype(jnp.int32)])
    left, right = turn(specimen, "mode", 1), turn(specimen, "mode", -1)
    cross = swap(edges(True, place, probe), 1)
    inner = swap(edges(False, place, probe), 0)
    *bands0, band1h, band1l, col = prepare(kernels, own)
    left, right, col = lax.optimization_barrier((left, right, col))
    far0, far1 = turn(left[0], "mode", 1), turn(right[1], "mode", -1)
    per = probe.shape[3] // PIECES // LANES
    far = PIECES - 1
    near_task = (0, tuple(range(far)), tuple(range(1, far * per - 1)))
    rest_tasks = (
        (0, (far,), tuple(range(far * per - 1, PIECES * per + 1))),
        (1, tuple(range(PIECES)), tuple(range(PIECES * per))),
    )
    blocks, lines = own_rows((near_task,), place, probe, [left, specimen, right], col)
    far0, far1, blocks, lines = lax.optimization_barrier((far0, far1, blocks, lines))

    def strips(specs, rows):
        last = jnp.stack([x[:, own - rows :] for x in specs])
        first = jnp.stack([x[:, :rows] for x in specs])
        inner = swap(jnp.where(odd == 1, first, last), 0)
        return swap(jnp.where(odd == 1, last, first), 1), inner

    strips0 = strips([left[0], specimen[0], right[0], far0], OUTER)
    strips1 = strips([left[1], specimen[1], right[1], far1], INNER)
    _, lines, edge_rows = own_rows(rest_tasks, place, probe, [left, specimen, right, far0], col, (cross, inner), (blocks, lines))
    wave = first_slice(place, edge_rows, strips0, (*bands0, col), lines)
    return second_slice(place, wave, (left, specimen, right, far1), strips1, (band1h, band1l, col), own)


def solution(mesh):
    return jax.shard_map(
        on_device,
        mesh=mesh,
        in_specs=(P("mode", None, "space", None), P(None, None, "space", "mode"), P()),
        out_specs=P("mode", None, "space", None),
        check_vma=False,
    )
```

```python
import functools

import jax
import jax.numpy as jnp
from jax import lax
from jax.experimental import pallas as pl
from jax.experimental.pallas import tpu as pltpu
from jax.sharding import PartitionSpec as P

TAPS = 24
HALF = TAPS // 2
LANES = 128
OUTER = 24
INNER = 16
PIECES = 4
MODE, ODD, UP, DOWN = range(4)
CHUNK = 512
GROUP = 4
f32 = jnp.float32
bf16 = jnp.bfloat16
VMEM = pl.BlockSpec(memory_space=pltpu.VMEM)
SMEM = pl.BlockSpec(memory_space=pltpu.SMEM)
HBM = pl.BlockSpec(memory_space=pltpu.HBM)


def in_hbm(x):
    return pltpu.with_memory_space_constraint(x, pltpu.HBM)


def in_vmem(x):
    return pltpu.with_memory_space_constraint(x, pltpu.VMEM)


def split(x):
    high = x.astype(bf16)
    return high, (x - high.astype(f32)).astype(bf16)


def look_up(tap, kernels, axis):
    real = jnp.zeros(tap.shape, f32)
    imag = jnp.zeros(tap.shape, f32)
    for t in range(TAPS):
        here = tap == t
        real = jnp.where(here, kernels[axis, 0, t], real)
        imag = jnp.where(here, kernels[axis, 1, t], imag)
    return real, imag


def position(index, own, edge):
    outer = index >= 2 * own
    line = jnp.where(outer, index - 2 * own, index)
    size = jnp.where(outer, 2 * edge, own)
    imag = line >= size
    line = jnp.where(imag, line - size, line)
    return jnp.where(outer, jnp.where(line < edge, line - edge, line - edge + own), line), imag


def row_band(kernels, own, out_edge, in_edge):
    shape = (2 * own + 4 * out_edge, 2 * own + 4 * in_edge)
    to, to_imag = position(lax.broadcasted_iota(jnp.int32, shape, 0), own, out_edge)
    at, at_imag = position(lax.broadcasted_iota(jnp.int32, shape, 1), own, in_edge)
    real, imag = look_up(at - to + HALF, kernels, 0)
    return split(jnp.where(to_imag == at_imag, real, jnp.where(to_imag, imag, -imag)))


def column_rows(source, is_imag, kernels):
    j = lax.broadcasted_iota(jnp.int32, source.shape, 1)
    real, imag = look_up(source - j + HALF, kernels, 1)
    left = jnp.where(is_imag, -imag, real)
    right = jnp.where(is_imag, real, imag)
    return split(left), split(right)


def tail_source(lane):
    is_imag = (lane >= 32) & (lane < 96)
    plain = jnp.where(is_imag, lane ^ 64, lane)
    source = jnp.where(plain < 64, plain + LANES, plain - LANES)
    inside = (plain < HALF) | (plain >= LANES - HALF)
    return jnp.where(inside, source, 1 << 20), is_imag


def edges_kernel(for_odd, place, probe, out, held, sems):
    odd = place[ODD]
    row = (odd if for_odd else 1 - odd) * (probe.shape[2] - OUTER)
    rows = pl.ds(pl.multiple_of(row, 8), OUTER)
    steps = [(m, p) for m in range(probe.shape[0]) for p in range(2)]
    takes = [pltpu.make_async_copy(probe.at[m, p, rows], held.at[m, p], sems.at[0, m, p]) for m, p in steps]
    gives = [pltpu.make_async_copy(held.at[m, p], out.at[m, p], sems.at[1, m, p]) for m, p in steps]
    for take in takes:
        take.start()
    for take, give in zip(takes, gives):
        take.wait()
        give.start()
    for give in gives:
        give.wait()


def edges(for_odd, place, probe):
    shape = (*probe.shape[:2], OUTER, probe.shape[3])
    return pl.pallas_call(
        functools.partial(edges_kernel, for_odd),
        out_shape=jax.ShapeDtypeStruct(shape, f32),
        in_specs=[SMEM, HBM],
        out_specs=HBM,
        scratch_shapes=[pltpu.VMEM(shape, f32), pltpu.SemaphoreType.DMA((2, shape[0], 2))],
        compiler_params=pltpu.CompilerParams(vmem_limit_bytes=4 * 1024 * 1024),
        name="edges_cross" if for_odd else "edges_inner",
    )(place, in_hbm(probe))


def prepare_kernel(kernels, row0h, row0l, row1h, row1l, col):
    own = row1h.shape[0] // 2
    row0h[...], row0l[...] = row_band(kernels, own, INNER, OUTER)
    row1h[...], row1l[...] = row_band(kernels, own, 0, INNER)
    lane = lax.broadcasted_iota(jnp.int32, (LANES, LANES), 0)
    for plane in range(2):
        left, right = column_rows(lane, jnp.full(lane.shape, plane == 1), kernels)
        for group, part in ((0, 0), (1, 0), (2, 1)):
            at = pl.ds((2 * group + plane) * LANES, LANES)
            col[at, :LANES] = left[part]
            col[at, LANES:] = right[part]
    source, is_imag = tail_source(lane)
    left, right = column_rows(source, is_imag, kernels)
    col[6 * LANES : 7 * LANES, :LANES] = left[0]
    col[6 * LANES : 7 * LANES, LANES:] = right[0]
    moved = (lane + LANES - 32) & (LANES - 1)
    source_moved, imag_moved = tail_source(moved)
    left_moved, right_moved = column_rows(source_moved, imag_moved, kernels)
    here = source < (1 << 19)
    col[7 * LANES :, :LANES] = jnp.where(here, left[0].astype(f32), left_moved[1].astype(f32)).astype(bf16)
    col[7 * LANES :, LANES:] = jnp.where(here, right[0].astype(f32), right_moved[1].astype(f32)).astype(bf16)


def prepare(kernels, own):
    mid = 2 * own + 4 * INNER
    shapes = [(mid, 2 * own + 4 * OUTER)] * 2 + [(2 * own, mid)] * 2 + [(8 * LANES, 2 * LANES)]
    return pl.pallas_call(
        prepare_kernel,
        out_shape=[pltpu.VMEM(s, bf16) for s in shapes],
        in_specs=[SMEM],
        out_specs=[VMEM] * 5,
        compiler_params=pltpu.CompilerParams(vmem_limit_bytes=8 * 1024 * 1024),
        name="prepare",
    )(kernels)


def dot(a, b):
    return jnp.dot(a, b, preferred_element_type=f32)


def row_stage(x_high, x_low, band_high, band_low):
    n = band_high.shape[0]
    both = dot(jnp.concatenate([band_high[...], band_low[...]], axis=0), x_high)
    return both[:n] + both[n:] + dot(band_high[...], x_low)


def product(f_real, f_imag, t_real, t_imag):
    return f_real * t_real - f_imag * t_imag, f_real * t_imag + f_imag * t_real


def lanes(block):
    return slice(block * LANES, (block + 1) * LANES)


def block_rows(j, rows, n=1):
    return slice(j * rows, (j + n) * rows)


def put(blocks, j, planes):
    rows, width = planes[0].shape
    for p, plane in enumerate(planes):
        high, low = split(plane)
        for b in range(width // LANES):
            at = block_rows(j + b, rows)
            blocks[at, lanes(p)] = high[:, lanes(b)]
            blocks[at, lanes(p + 2)] = low[:, lanes(b)]


def joined(place, piece):
    return jnp.where(lax.rem(place[MODE] + piece + PIECES - 1, PIECES) == PIECES - 1, 0.0, 1.0)


def column_stage(place, blocks, tails, col, js, rows, emit):
    total = blocks.shape[0] // rows
    per = total // PIECES
    lane = lax.broadcasted_iota(jnp.int16, (rows, LANES), 1)
    plain = lane & 63
    middle = (lane >= 32) & (lane < 96)
    used = (plain < HALF) | (plain >= 64 - HALF)

    def beside(j, step, k):
        x = blocks[block_rows((j + step) % total, rows), lanes(k)]
        if (j + (step > 0)) % per:
            return x
        keep = joined(place, (j // per - (step < 0)) % PIECES)
        return (x.astype(f32) * keep).astype(bf16)

    for n, j in enumerate(js):
        side = [jnp.where(lane < 64, beside(j, 1, k), beside(j, -1, k)) for k in range(4)]
        high = jnp.where(middle, pltpu.roll(side[1], 64, 1), side[0])
        low = jnp.where(middle, pltpu.roll(side[3], 64, 1), side[2])
        tails[block_rows(n, rows), lanes(0)] = high
        tails[block_rows(n, rows), lanes(1)] = jnp.where(used, low, pltpu.roll(high, 32, 1))
    two = 2 * LANES
    done = 0
    while done < len(js):
        first = js[done] % total
        n = min(len(js) - done, total - first, GROUP)
        at = block_rows(first, rows, n)
        main = blocks[at, :two]
        result = dot(main, col[:two, :]) + dot(blocks[at, two:], col[two : 2 * two, :])
        result = result + dot(main, col[2 * two : 3 * two, :]) + dot(tails[block_rows(done, rows, n), :], col[3 * two :, :])
        for b in range(n):
            part = result[block_rows(b, rows)]
            emit(first + b, part[:, :LANES], part[:, LANES:])
        done += n


def chunks(width):
    return [slice(c, c + CHUNK) for c in range(0, width, CHUNK)]


def keep_columns(lines, rows):
    def emit(j, real, imag):
        for p, plane in enumerate((real, imag)):
            for k, part in enumerate(split(plane)):
                lines[k, p * rows : (p + 1) * rows, lanes(j)] = part

    return emit


def piece_columns(place, q, piece):
    return pl.ds(pl.multiple_of(lax.rem(place[MODE] + q + PIECES - 1, PIECES) * piece, piece), piece)


def own_product(fields, spec, blocks, q, at, piece):
    cells = slice(q * piece + at.start, q * piece + at.stop)
    planes = product(fields[0, :, at], fields[1, :, at], *(x[:, at].astype(f32) for x in spec))
    put(blocks, cells.start // LANES, planes)


def own_kernel(tasks, edges_too, place, probe, *refs):
    n = 1 + max(q for _, pieces, _ in tasks for q in pieces)
    specs, col = refs[:n], refs[n]
    if edges_too:
        cross, inner = refs[n + 1 : n + 3]
        blocks, lines, edge_rows, fields, tails, sems, edge_sems = refs[n + 5 :]
    else:
        blocks, lines, fields, tails, sems = refs[n + 1 :]
    modes, _, rows, width = probe.shape
    piece = width // PIECES
    odd = place[ODD]

    def fetch(k, m, q):
        return pltpu.make_async_copy(probe.at[m, :, :, piece_columns(place, q, piece)], fields.at[k], sems.at[k])

    order = [(m, q) for m, pieces, _ in tasks for q in pieces]
    for k, (m, q) in enumerate(order):
        fetch(k, m, q).start()
    copies = []
    if edges_too:
        for m in range(modes):
            for q in range(PIECES):
                at = piece_columns(place, q, piece)
                for e, (source, to) in enumerate(((cross, odd), (inner, 1 - odd))):
                    copies.append(pltpu.make_async_copy(source.at[m, :, :, at], edge_rows.at[to, m, q], edge_sems.at[e, m, q]))
    for copy in copies:
        copy.start()
    k = 0
    for t, (m, pieces, js) in enumerate(tasks):
        for q in pieces:
            fetch(k, m, q).wait()
            spec = [specs[q].at[0, p] if q < PIECES - 1 else specs[q].at[p] for p in range(2)]
            for at in chunks(piece):
                own_product(fields.at[k], spec, blocks.at[m], q, at, piece)
            k += 1
        column_stage(place, blocks.at[m], tails.at[t], col, js, rows, keep_columns(lines.at[m], rows))
    for copy in copies:
        copy.wait()


def own_rows(tasks, place, probe, specs, col, halos=(), made=()):
    modes, _, own, width = probe.shape
    args = [in_hbm(probe)] + [in_vmem(x) for x in (*specs, col)] + [*halos] + [in_vmem(x) for x in made]
    piece = width // PIECES
    fetches = sum(len(pieces) for _, pieces, _ in tasks)
    longest = max(len(js) for _, _, js in tasks)
    out = [
        pltpu.VMEM((modes, width // LANES * own, 4 * LANES), bf16),
        pltpu.VMEM((modes, 2, 2 * own, width), bf16),
    ]
    scratch = [
        pltpu.VMEM((fetches, 2, own, piece), f32),
        pltpu.VMEM((len(tasks), longest * own, 2 * LANES), bf16),
        pltpu.SemaphoreType.DMA((fetches,)),
    ]
    if halos:
        out.append(pltpu.VMEM((2, modes, PIECES, 2, OUTER, piece), f32))
        scratch.append(pltpu.SemaphoreType.DMA((2, modes, PIECES)))
    first = 1 + len(args) - len(made)
    return pl.pallas_call(
        functools.partial(own_kernel, tasks, bool(halos)),
        out_shape=out,
        in_specs=[SMEM, HBM] + [VMEM] * (1 + len(specs)) + [pl.BlockSpec(memory_space=pl.ANY)] * len(halos) + [VMEM] * len(made),
        out_specs=[VMEM] * len(out),
        input_output_aliases={first + k: k for k in range(len(made))},
        scratch_shapes=scratch,
        compiler_params=pltpu.CompilerParams(vmem_limit_bytes=20 * 1024 * 1024),
        cost_estimate=pl.CostEstimate(flops=4 * 10**9, bytes_accessed=10**7, transcendentals=0),
        name="own_rest" if halos else "own_near",
    )(place, *args)


def first_kernel(place, edge_rows, strips_cross, strips_inner, high, low, col, lines, wave, strips, outer, outer_lines, outer_tails, strip_sems):
    _, modes, _, _, _, piece = edge_rows.shape
    width = PIECES * piece
    edge = 2 * OUTER
    odd = place[ODD]
    keep = [place[UP].astype(f32), place[DOWN].astype(f32)]
    strip_copies = [
        pltpu.make_async_copy(source, strips.at[to], strip_sems.at[to])
        for source, to in ((strips_cross, odd), (strips_inner, 1 - odd))
    ]
    for copy in strip_copies:
        copy.start()
    for copy in strip_copies:
        copy.wait()
    for m in range(modes):
        for q in range(PIECES):
            for at in chunks(piece):
                planes = [
                    product(*(edge_rows[e, m, q, p, :, at] for p in range(2)), *(strips[e, q, p, :, at].astype(f32) * keep[e] for p in range(2)))
                    for e in range(2)
                ]
                put(outer.at[m], (q * piece + at.start) // LANES, [jnp.concatenate([planes[0][p], planes[1][p]], axis=0) for p in range(2)])
    for m in range(modes):
        column_stage(place, outer.at[m], outer_tails.at[m], col, list(range(width // LANES)), edge, keep_columns(outer_lines.at[m], edge))
    for m in range(modes):
        for at in chunks(width):
            x = [jnp.concatenate([lines[m, k, :, at], outer_lines[m, k, :, at]], axis=0) for k in range(2)]
            wave[m, :, at] = row_stage(*x, high, low)


def first_slice(place, edge_rows, strips, bands, lines):
    modes = lines.shape[0]
    width = lines.shape[3]
    args = [in_vmem(edge_rows), *strips] + [in_vmem(x) for x in (*bands, lines)]
    edge = 2 * OUTER
    total = width // LANES
    return pl.pallas_call(
        first_kernel,
        out_shape=pltpu.VMEM((modes, bands[0].shape[0], width), f32),
        in_specs=[SMEM, VMEM] + [pl.BlockSpec(memory_space=pl.ANY)] * 2 + [VMEM] * (1 + len(bands)),
        out_specs=VMEM,
        scratch_shapes=[
            pltpu.VMEM((2, *strips[0].shape), bf16),
            pltpu.VMEM((modes, total * edge, 4 * LANES), bf16),
            pltpu.VMEM((modes, 2, 2 * edge, width), bf16),
            pltpu.VMEM((modes, total * edge, 2 * LANES), bf16),
            pltpu.SemaphoreType.DMA((2,)),
        ],
        compiler_params=pltpu.CompilerParams(vmem_limit_bytes=24 * 1024 * 1024),
        name="first_slice",
    )(place, *args)


def second_kernel(place, wave, left, own_spec, right, far_spec, strips_cross, strips_inner, high, low, col, out, blocks, tails, stage, strips, sems, strip_sems):
    modes, _, rows, width = out.shape
    piece = width // PIECES
    per = piece // LANES
    keep = [place[UP].astype(f32), place[DOWN].astype(f32)]
    specs = [[x.at[1, p] for p in range(2)] for x in (left, own_spec, right)] + [[far_spec.at[0], far_spec.at[1]]]
    odd = place[ODD]
    strip_copies = [
        pltpu.make_async_copy(source, strips.at[to], strip_sems.at[to])
        for source, to in ((strips_cross, odd), (strips_inner, 1 - odd))
    ]
    for copy in strip_copies:
        copy.start()
    for copy in strip_copies:
        copy.wait()

    def leave(m, q):
        at = slice(q * piece, (q + 1) * piece)
        return pltpu.make_async_copy(stage.at[m, :, :, at], out.at[m, :, :, piece_columns(place, q, piece)], sems.at[m, q])

    for m in range(modes):
        for q in range(PIECES):
            for at in chunks(piece):
                cells = slice(q * piece + at.start, q * piece + at.stop)
                inside = product(wave[m, :rows, cells], wave[m, rows : 2 * rows, cells], *(x[:, at].astype(f32) for x in specs[q]))
                edge = [jnp.concatenate([strips[e, q, p, :, at].astype(f32) * keep[e] for e in range(2)], axis=0) for p in range(2)]
                first = 2 * rows
                outside = product(wave[m, first : first + 2 * INNER, cells], wave[m, first + 2 * INNER :, cells], *edge)
                result = row_stage(*split(jnp.concatenate([*inside, *outside], axis=0)), high, low)
                put(blocks.at[m], cells.start // LANES, (result[:rows], result[rows:]))

    for m in range(modes):

        def emit(j, real, imag, m=m):
            stage[m, 0, :, lanes(j)] = real
            stage[m, 1, :, lanes(j)] = imag
            if j % per == per - 1:
                leave(m, j // per).start()

        column_stage(place, blocks.at[m], tails.at[m], col, list(range(PIECES * per)), rows, emit)
    for m in range(modes):
        for q in range(PIECES):
            leave(m, q).wait()


def second_slice(place, wave, specs, strips, bands, own):
    modes, _, width = wave.shape
    args = [*(in_vmem(x) for x in (wave, *specs)), *strips, *(in_vmem(x) for x in bands)]
    shape = (modes, 2, own, width)
    total = width // LANES
    return pl.pallas_call(
        second_kernel,
        out_shape=jax.ShapeDtypeStruct(shape, f32),
        in_specs=[SMEM] + [VMEM] * (1 + len(specs)) + [pl.BlockSpec(memory_space=pl.ANY)] * 2 + [VMEM] * len(bands),
        out_specs=HBM,
        scratch_shapes=[
            pltpu.VMEM((modes, total * own, 4 * LANES), bf16),
            pltpu.VMEM((modes, total * own, 2 * LANES), bf16),
            pltpu.VMEM(shape, f32),
            pltpu.VMEM((2, *strips[0].shape), bf16),
            pltpu.SemaphoreType.DMA((modes, PIECES)),
            pltpu.SemaphoreType.DMA((2,)),
        ],
        compiler_params=pltpu.CompilerParams(vmem_limit_bytes=28 * 1024 * 1024),
        name="second_slice",
    )(place, *args)


def turn(x, axis, by):
    n = lax.axis_size(axis)
    return lax.ppermute(x, axis, [(i, (i + by) % n) for i in range(n)])


def swap(x, first):
    n = lax.axis_size("space")
    pairs = [(i, i + 1) for i in range(first, n - 1, 2)]
    return lax.ppermute(x, "space", pairs + [(j, i) for i, j in pairs])


def on_device(probe, specimen, kernels):
    own = probe.shape[2]
    space, mode = lax.axis_index("space"), lax.axis_index("mode")
    odd = space % 2
    place = jnp.stack([mode, odd, (space > 0).astype(jnp.int32), (space < lax.axis_size("space") - 1).astype(jnp.int32)])
    left, right = turn(specimen, "mode", 1), turn(specimen, "mode", -1)
    cross = swap(edges(True, place, probe), 1)
    inner = swap(edges(False, place, probe), 0)
    *bands0, band1h, band1l, col = prepare(kernels, own)
    left, right, col = lax.optimization_barrier((left, right, col))
    far0, far1 = turn(left[0], "mode", 1), turn(right[1], "mode", -1)
    per = probe.shape[3] // PIECES // LANES
    far = PIECES - 1
    near_task = (0, tuple(range(far)), tuple(range(1, far * per - 1)))
    rest_tasks = (
        (0, (far,), tuple(range(far * per - 1, PIECES * per + 1))),
        (1, tuple(range(PIECES)), tuple(range(PIECES * per))),
    )
    blocks, lines = own_rows((near_task,), place, probe, [left, specimen, right], col)
    far0, far1, blocks, lines = lax.optimization_barrier((far0, far1, blocks, lines))

    def strips(specs, rows):
        last = jnp.stack([x[:, own - rows :] for x in specs])
        first = jnp.stack([x[:, :rows] for x in specs])
        inner = swap(jnp.where(odd == 1, first, last), 0)
        return swap(jnp.where(odd == 1, last, first), 1), inner

    strips0 = strips([left[0], specimen[0], right[0], far0], OUTER)
    strips1 = strips([left[1], specimen[1], right[1], far1], INNER)
    _, lines, edge_rows = own_rows(rest_tasks, place, probe, [left, specimen, right, far0], col, (cross, inner), (blocks, lines))
    wave = first_slice(place, edge_rows, strips0, (*bands0, col), lines)
    return second_slice(place, wave, (left, specimen, right, far1), strips1, (band1h, band1l, col), own)


def solution(mesh):
    return jax.shard_map(
        on_device,
        mesh=mesh,
        in_specs=(P("mode", None, "space", None), P(None, None, "space", "mode"), P()),
        out_specs=P("mode", None, "space", None),
        check_vma=False,
    )
```
